32 devices in a mesh: ctx: 4 (over z), ep: 8 (over y, x, core).
Axes of the slice: x: 2, y: 2, z: 4, core: 2. Of those that a mesh axis runs over, the one named last changes fastest.
Arguments:
- queries: bfloat16 [1024, 8192], P('ctx', 'ep'), may hold values from -6 to 6
- key_rows: bfloat16 [1024, 8192], P('ctx', 'ep'), may hold values from -6 to 6
- value_rows: bfloat16 [1024, 8192], P('ctx', 'ep'), may hold values from -6 to 6
- log_decay: float32 [1024, 64], P('ctx', 'ep'), may hold values from -1 to 0
- out_weight: bfloat16 [6144, 8192], P('ep'), may hold values from -0.0625 to 0.0625
- expert_ids: int32 [1024, 2], P('ctx'), may hold values from 0 to 7, all different within a row; in each aligned block of 256 rows (0 to 255, 256 to 511, ...) at most 128 rows name the same one
- flagged: int32 [256], P('ctx'), may hold values from 0 to 1023, as said below
- direction: float32 [6144], P('ep'), as said below
Outputs:
- expert_tiles: bfloat16 [8, 512, 6144], P('ep', 'ctx')
The draws below stay inside these ranges and needn't reach their ends.
Inputs may be any that keep to these rules, and one draw needn't show every extreme that they name: `expert_ids`: each row names 2 different experts; among the 256 rows of one block of the sequence no expert is named more than 128 times, a bound that some block reaches. `flagged`: entries 64 * b to 64 * b + 63 are distinct rows of block b of 256 rows. `direction`: not all zero.
All inputs are finite; a program needn't handle non-finite values.
Results may differ from the reference program's by a relative error of at most 0.0059.
Values may be sent and summed in bfloat16 or wider, within the bound.
A program may use at most 64 MiB of HBM per device.

```python
import math
import jax
import jax.numpy as jnp
import numpy as np
from jax import lax

MODEL = 6144
HEAD_COUNT = 64
HEAD = 128
TOP = 2
SUB = 256
ROWS_PER_BLOCK = 256
FLAG_DEV = 64
EXPERTS = 8
SEQUENCE_LENGTH = 1024
CAP = 128
N_CTX = 4


def draw_log_decay(key, part):
    key_sequence = jax.random.split(key, 6)
    head_pick = jax.random.uniform(key_sequence[0], (HEAD_COUNT,))
    fast_share = 0.5
    quick_decay_heads = head_pick < fast_share
    fast_rate = math.log(10.0) / (30.0 + 20.0 * jax.random.uniform(key_sequence[1], (HEAD_COUNT,)))
    slow_rate = math.log(2.0) / SEQUENCE_LENGTH
    base_rate = jnp.where(quick_decay_heads, fast_rate, slow_rate)
    every_block = SEQUENCE_LENGTH // ROWS_PER_BLOCK
    low_end = -math.log(2.0)
    high_end = math.log(2.0)
    block_factor = jnp.exp(jax.random.uniform(key_sequence[2], (every_block, 1, HEAD_COUNT), minval=low_end, maxval=high_end))
    position_factor = jnp.exp(jax.random.uniform(key_sequence[3], (every_block, ROWS_PER_BLOCK, HEAD_COUNT), minval=low_end, maxval=high_end))
    rate_all = base_rate[None, None, :] * block_factor * position_factor
    spike_events = jax.random.uniform(key_sequence[4], (every_block, ROWS_PER_BLOCK, HEAD_COUNT)) < 3.0 / SEQUENCE_LENGTH
    spike_falloff = jnp.log(jax.random.uniform(key_sequence[5], (every_block, ROWS_PER_BLOCK, HEAD_COUNT), minval=0.5, maxval=0.8))
    skipped_ahead = jnp.where(spike_events & jnp.logical_not(quick_decay_heads)[None, None, :], spike_falloff, 0.0)
    return (skipped_ahead - rate_all).reshape(SEQUENCE_LENGTH, HEAD_COUNT).astype(jnp.float32)


def draw_flagged(key, part):
    every_block = SEQUENCE_LENGTH // ROWS_PER_BLOCK
    key_sequence = jax.random.split(key, every_block)

    def choose_rows(block_key):
        order = jax.random.permutation(block_key, ROWS_PER_BLOCK).astype(jnp.int32)
        return ((order - order[0]) % ROWS_PER_BLOCK)[:FLAG_DEV]
    chosen = jax.vmap(choose_rows)(key_sequence).astype(jnp.int32)
    block_index = jnp.arange(every_block, dtype=jnp.int32)[:, None]
    mirrored = jnp.where(block_index % 2 == 1, ROWS_PER_BLOCK - 1 - chosen, chosen)
    starts = block_index * ROWS_PER_BLOCK
    return (mirrored + starts).reshape(-1).astype(jnp.int32)


def draw_direction(key, part):
    key_sequence = jax.random.split(key, 2)
    width = MODEL
    magnitude = jnp.exp(jax.random.uniform(key_sequence[0], (width,)) * math.log(64.0))
    signed = jax.random.normal(key_sequence[1], (width,))
    return (signed * magnitude / 16.0).astype(jnp.float32)


def levels(own_key, dims, cuts, low, high):
    gain = 1.0
    for position, parts in cuts:
        steps = jax.random.uniform(jax.random.fold_in(jax.random.fold_in(own_key, 6), position), (parts,), jnp.float32, low / len(cuts), high / len(cuts))
        gain = gain * jnp.repeat(jnp.exp(steps), dims[position] // parts).reshape((-1,) + (1,) * (len(dims) - 1 - position))
    return gain


def routed_block(own_key, own, number, rows, amount, top, most, skew):
    sequence = jax.random.permutation(own_key, amount)
    heavy_load, common = portions_of(amount, rows * top, most, skew, True), portions_of(amount, rows * top, most, skew, False)
    places = jnp.arange(amount)

    def named(tallies, offset_by):
        used = int((tallies > 0).sum())
        fixed = max(1, used // 4)
        shifted = fixed + (places - fixed + offset_by * (used - fixed)) % max(1, amount - fixed)
        return jnp.zeros((amount,), jnp.int32).at[sequence[jnp.where(places < fixed, places, shifted)]].set(jnp.asarray(tallies, jnp.int32))

    tallies = jnp.where(number % 4 == 0, named(heavy_load, number // 4), named(common, number - number // 4 - 1))
    mixed = jax.random.permutation(jax.random.fold_in(own, 3), amount)
    source_of, receiver = mixed[0:amount // 2 * 2:2], mixed[1:amount // 2 * 2:2]
    room = jnp.minimum(tallies[source_of] - 1, most - tallies[receiver]) // 2
    room = jnp.where((source_of == sequence[0]) | (receiver == sequence[0]) | (tallies[receiver] == 0), 0, jnp.maximum(room, 0))
    shifted = jax.random.randint(jax.random.fold_in(own, 4), (amount // 2,), 0, 1 << 20) % (room + 1)
    tallies = tallies.at[source_of].add(-shifted).at[receiver].add(shifted)
    labels = jnp.searchsorted(jnp.cumsum(tallies), jnp.arange(rows * top), side="right").astype(jnp.int32)
    listing = labels.reshape(top, rows).T
    listing = listing[jax.random.permutation(jax.random.fold_in(own, 1), rows)]
    offset_by = jax.random.randint(jax.random.fold_in(own, 2), (rows, 1), 0, top)
    return jnp.take_along_axis(listing, (jnp.arange(top)[None, :] + offset_by) % top, axis=1)


def portions_of(amount, total, limit, skew, full):
    loads = [(1 << 20) // math.isqrt(standing ** skew) + 1 for standing in range(1, amount + 1)]
    largest = limit if full else min(limit, max(-(-total // amount), total * loads[0] // sum(loads)))
    least = 1 if total - largest >= amount - 1 else 0
    given, spare = [largest] + [least] * (amount - 1), total - largest - least * (amount - 1)
    while spare > 0:
        candidates = [i for i in range(1, amount) if given[i] < largest] or [i for i in range(1, amount) if given[i] < limit]
        pool, remaining = sum([loads[i] for i in candidates]), spare
        for i in candidates:
            addition = min(limit - given[i], max(1, remaining * loads[i] // pool), spare)
            given[i] = given[i] + addition
            spare = spare - addition
    return np.array(given)


def bell_draw(key, dims, deviation, reach, cuts=(), kind=jnp.bfloat16):
    result = deviation * jax.random.normal(key, dims, jnp.float32)
    if cuts:
        result = result * levels(key, dims, cuts, -0.22, 0.18)
    return jnp.clip(result, -reach, reach).astype(kind)


def setup_inputs(seed: int = 0) -> dict:
    streams_of = jax.random.split(jax.random.key(seed), 9)
    queries = bell_draw(streams_of[0], (SEQUENCE_LENGTH, HEAD_COUNT * HEAD), 1.0, 6.0, ((0, 4), (1, 8)))
    key_rows = bell_draw(streams_of[1], (SEQUENCE_LENGTH, HEAD_COUNT * HEAD), 1.0, 6.0, ((0, 4), (1, 8)))
    value_rows = bell_draw(streams_of[2], (SEQUENCE_LENGTH, HEAD_COUNT * HEAD), 1.0, 6.0, ((0, 4), (1, 8)))
    log_decay = draw_log_decay(jax.random.fold_in(streams_of[8], 71), 0)
    out_weight = bell_draw(streams_of[4], (MODEL, HEAD_COUNT * HEAD), (HEAD_COUNT * HEAD) ** -0.5, 0.0625, ((0, 8),))
    expert_ids_keys = jax.random.split(jax.random.fold_in(streams_of[5], 1), SEQUENCE_LENGTH // ROWS_PER_BLOCK)
    expert_ids_turns = jax.random.permutation(jax.random.fold_in(streams_of[5], 3), SEQUENCE_LENGTH // ROWS_PER_BLOCK)
    expert_ids = jax.vmap(lambda own, number: routed_block(jax.random.fold_in(streams_of[5], 2), own, number, ROWS_PER_BLOCK, EXPERTS, TOP, CAP, 1))(expert_ids_keys, expert_ids_turns).reshape((SEQUENCE_LENGTH, TOP))
    flagged = draw_flagged(jax.random.fold_in(streams_of[8], 71), 0)
    direction = draw_direction(jax.random.fold_in(streams_of[8], 71), 0)
    return dict(queries=queries, key_rows=key_rows, value_rows=value_rows, log_decay=log_decay, out_weight=out_weight, expert_ids=expert_ids, flagged=flagged, direction=direction)


def sub_step(kv_state, pieces):
    query_sub, key_sub, value_sub, decay_sub = pieces
    cumulated = jnp.cumsum(decay_sub, axis=0)
    scores = jnp.einsum('thd,shd->hts', query_sub.astype(jnp.float32), key_sub.astype(jnp.float32))
    spread = jnp.transpose(cumulated)
    decay_gaps = jnp.minimum(spread[:, :, None] - spread[:, None, :], 0.0)
    causal = jnp.arange(SUB, dtype=jnp.int32)[:, None] >= jnp.arange(SUB, dtype=jnp.int32)[None, :]
    weights = jnp.where(causal[None], scores * jnp.exp(decay_gaps), 0.0).astype(jnp.bfloat16)
    inside = jnp.einsum('hts,shd->thd', weights.astype(jnp.float32), value_sub.astype(jnp.float32))
    scaled = query_sub.astype(jnp.float32) * jnp.exp(cumulated)[:, :, None]
    carried = jnp.einsum('thd,hde->the', scaled, kv_state, precision=lax.Precision.HIGHEST)
    last_decay = cumulated[-1]
    key_scaled = (key_sub.astype(jnp.float32) * jnp.exp(last_decay[None, :] - cumulated)[:, :, None]).astype(jnp.bfloat16)
    update = jnp.einsum('shd,she->hde', key_scaled.astype(jnp.float32), value_sub.astype(jnp.float32))
    kv_state = jnp.exp(last_decay)[:, None, None] * kv_state + update
    return (kv_state, inside + carried)

def normalize(outputs):
    mean_square = lax.optimization_barrier(jnp.mean(outputs * outputs, axis=-1, keepdims=True))
    return (outputs * lax.rsqrt(mean_square + 1e-06)).astype(jnp.bfloat16)

def reference(queries, key_rows, value_rows, log_decay, out_weight, expert_ids, flagged, direction):
    sub_count = SEQUENCE_LENGTH // SUB

    def shaped(operand):
        return operand.reshape(sub_count, SUB, HEAD_COUNT, HEAD)
    start_state = jnp.zeros((HEAD_COUNT, HEAD, HEAD), jnp.float32)
    final_state, outputs = lax.scan(sub_step, start_state, (shaped(queries), shaped(key_rows), shaped(value_rows), log_decay.reshape(sub_count, SUB, HEAD_COUNT)))
    attended = normalize(outputs).reshape(SEQUENCE_LENGTH, HEAD_COUNT * HEAD)
    projected = lax.dot_general(attended, out_weight, (((1,), (1,)), ((), ())), preferred_element_type=jnp.float32).astype(jnp.bfloat16)
    norm_square = jnp.sum(direction * direction) + 1e-06
    picked = projected[flagged].astype(jnp.float32)
    products = jnp.dot(picked, direction, precision=lax.Precision.HIGHEST)
    removed = (picked - (products / norm_square)[:, None] * direction[None, :]).astype(jnp.bfloat16)
    ablated = projected.at[flagged].set(removed)
    grouped = expert_ids.reshape(N_CTX, ROWS_PER_BLOCK * TOP)
    matches = (grouped[:, :, None] == jnp.arange(EXPERTS, dtype=jnp.int32)[None, None, :]).astype(jnp.int32)
    slot_index = lax.optimization_barrier(jnp.sum((jnp.cumsum(matches, axis=1) - matches) * matches, axis=2)).reshape(-1)
    source = jnp.arange(SEQUENCE_LENGTH * TOP, dtype=jnp.int32) // TOP
    positions = source // ROWS_PER_BLOCK * CAP + slot_index
    tile_rows = jnp.zeros((EXPERTS, N_CTX * CAP, MODEL), jnp.bfloat16)
    return tile_rows.at[expert_ids.reshape(-1), positions].set(ablated[source])
```

```python
import jax
import jax.numpy as jnp
from jax import lax
from jax.sharding import PartitionSpec as P

HEAD = 128
TOP = 2
EXP_DEV = 1
SUB = 256


def passed_along(value, axis, steps):
    count = lax.axis_size(axis)
    leading, last = (max(0, -steps), min(count, count - steps))
    return lax.ppermute(value, axis, [(source, source + steps) for source in range(leading, last)])


def local_step(carried_in, pieces):
    kv_state, offset = carried_in
    query_sub, key_sub, value_sub, decay_sub = pieces
    sub_rows = query_sub.shape[0]
    cumulated = jnp.cumsum(decay_sub, axis=0)
    scores = jnp.einsum("thd,shd->hts", query_sub, key_sub, preferred_element_type=jnp.float32)
    spread = jnp.transpose(cumulated)
    decay_gaps = jnp.minimum(spread[:, :, None] - spread[:, None, :], 0.0)
    causal = (
        jnp.arange(sub_rows, dtype=jnp.int32)[:, None]
        >= jnp.arange(sub_rows, dtype=jnp.int32)[None, :]
    )
    weights = jnp.where(causal[None], scores * jnp.exp(decay_gaps), 0.0).astype(jnp.bfloat16)
    inside = jnp.einsum("hts,shd->thd", weights, value_sub, preferred_element_type=jnp.float32)
    scaled = query_sub.astype(jnp.float32) * jnp.exp(cumulated)[:, :, None]
    carried = jnp.einsum("thd,hde->the", scaled, kv_state, precision=lax.Precision.HIGHEST)
    last_decay = cumulated[-1]
    key_scaled = (
        key_sub.astype(jnp.float32) * jnp.exp(last_decay[None, :] - cumulated)[:, :, None]
    ).astype(jnp.bfloat16)
    update = jnp.einsum("shd,she->hde", key_scaled, value_sub, preferred_element_type=jnp.float32)
    kv_state = jnp.exp(last_decay)[:, None, None] * kv_state + update
    reach_decay = jnp.exp(offset[None, :] + cumulated)
    return ((kv_state, offset + last_decay), (inside + carried, reach_decay))


def normalize(outputs):
    mean_square = jnp.mean(outputs * outputs, axis=-1, keepdims=True)
    return (outputs * lax.rsqrt(mean_square + 1e-06)).astype(jnp.bfloat16)


def local(queries, key_rows, value_rows, log_decay, out_weight, expert_ids, flagged, direction):
    block_rows = queries.shape[0]
    local_width = queries.shape[1]
    local_heads = local_width // HEAD
    sub_count = block_rows // SUB
    model_cols = out_weight.shape[0]

    def shaped(operand):
        return operand.reshape(sub_count, SUB, local_heads, HEAD)

    start_state = (
        jnp.zeros((local_heads, HEAD, HEAD), jnp.float32),
        jnp.zeros((local_heads,), jnp.float32),
    )
    scanned = lax.scan(
        local_step,
        start_state,
        (
            shaped(queries),
            shaped(key_rows),
            shaped(value_rows),
            log_decay.reshape(sub_count, SUB, local_heads),
        ),
    )
    local_state, total_decay = scanned[0]
    partial_out, reach_decay = scanned[1]
    block_gain = jnp.exp(total_decay)

    def pass_state(hop_index, incoming):
        passed = block_gain[:, None, None] * incoming + local_state
        return passed_along(passed.astype(jnp.bfloat16), "ctx", 1).astype(jnp.float32)

    incoming = lax.fori_loop(0, lax.axis_size("ctx") - 1, pass_state, jnp.zeros_like(local_state))
    scaled = shaped(queries).astype(jnp.float32) * reach_decay[..., None]
    outputs = partial_out + jnp.einsum(
        "cthd,hde->cthe", scaled, incoming, precision=lax.Precision.HIGHEST
    )
    attended = normalize(outputs).reshape(block_rows, local_width)
    projected = lax.dot_general(
        lax.all_gather(attended, "ep", axis=1, tiled=True),
        out_weight,
        (((1,), (1,)), ((), ())),
        preferred_element_type=jnp.float32,
    ).astype(jnp.bfloat16)
    ctx_start = lax.axis_index("ctx") * block_rows
    local_flags = flagged - ctx_start
    experts_all = lax.axis_size("ep") * EXP_DEV
    capacity = 2 * block_rows * TOP // experts_all
    row_number = jnp.arange(block_rows, dtype=jnp.int32)
    expert_number = jnp.arange(experts_all, dtype=jnp.int32)
    named = jnp.any(expert_ids[:, :, None] == expert_number[None, None, :], axis=1)
    before = (row_number[:, None] > row_number[None, :]).astype(jnp.bfloat16)
    slot_index = jnp.dot(before, named.astype(jnp.bfloat16), preferred_element_type=jnp.float32)
    slot_index = jnp.where(named, slot_index.astype(jnp.int32), -1).T
    picks = slot_index[:, None, :] == jnp.arange(capacity, dtype=jnp.int32)[None, :, None]
    tile_rows = jnp.einsum(
        "ecr,rm->ecm",
        picks.astype(jnp.bfloat16),
        projected,
        preferred_element_type=jnp.float32,
    ).astype(jnp.bfloat16)
    tiles = lax.all_to_all(tile_rows, "ep", split_axis=0, concat_axis=2, tiled=True)
    row_flags = jnp.any(local_flags[:, None] == row_number[None, :], axis=0)
    own_picks = lax.dynamic_slice_in_dim(picks, lax.axis_index("ep") * EXP_DEV, EXP_DEV, 0)
    slot_flags = jnp.any(own_picks & row_flags[None, None, :], axis=2)
    whole_direction = lax.all_gather(direction, "ep", tiled=True)
    norm_square = jnp.sum(whole_direction * whole_direction) + 1e-06
    rows = tiles.astype(jnp.float32)
    products = jnp.sum(rows * whole_direction, axis=2)
    removed = rows - (products / norm_square)[:, :, None] * whole_direction
    return jnp.where(slot_flags[:, :, None], removed.astype(jnp.bfloat16), tiles)


def solution(mesh):
    placed = (
        P("ctx", "ep"),
        P("ctx", "ep"),
        P("ctx", "ep"),
        P("ctx", "ep"),
        P("ep", None),
        P("ctx", None),
        P("ctx"),
        P("ep"),
    )
    return jax.shard_map(
        local, mesh=mesh, in_specs=placed, out_specs=P("ep", "ctx", None), check_vma=False
    )
```

```python
import functools

import jax
import jax.numpy as jnp
from jax import lax
from jax.experimental import pallas as pl
from jax.experimental.pallas import tpu as pltpu
from jax.sharding import PartitionSpec as P

HEAD = 128
TOP = 2
EXP_DEV = 1
SUB = 256
MESH = pl.DeviceIdType.MESH


def passed_along(value, axis, steps):
    count = lax.axis_size(axis)
    leading, last = (max(0, -steps), min(count, count - steps))
    return lax.ppermute(value, axis, [(source, source + steps) for source in range(leading, last)])


def local_step(carried_in, pieces):
    kv_state, offset = carried_in
    query_sub, key_sub, value_sub, decay_sub = pieces
    sub_rows = query_sub.shape[0]
    cumulated = jnp.cumsum(decay_sub, axis=0)
    scores = jnp.einsum("thd,shd->hts", query_sub, key_sub, preferred_element_type=jnp.float32)
    spread = jnp.transpose(cumulated)
    decay_gaps = jnp.minimum(spread[:, :, None] - spread[:, None, :], 0.0)
    causal = (
        jnp.arange(sub_rows, dtype=jnp.int32)[:, None]
        >= jnp.arange(sub_rows, dtype=jnp.int32)[None, :]
    )
    weights = jnp.where(causal[None], scores * jnp.exp(decay_gaps), 0.0).astype(jnp.bfloat16)
    inside = jnp.einsum("hts,shd->thd", weights, value_sub, preferred_element_type=jnp.float32)
    scaled = query_sub.astype(jnp.float32) * jnp.exp(cumulated)[:, :, None]
    carried = jnp.einsum("thd,hde->the", scaled, kv_state, precision=lax.Precision.HIGHEST)
    last_decay = cumulated[-1]
    key_scaled = (
        key_sub.astype(jnp.float32) * jnp.exp(last_decay[None, :] - cumulated)[:, :, None]
    ).astype(jnp.bfloat16)
    update = jnp.einsum("shd,she->hde", key_scaled, value_sub, preferred_element_type=jnp.float32)
    kv_state = jnp.exp(last_decay)[:, None, None] * kv_state + update
    reach_decay = jnp.exp(offset[None, :] + cumulated)
    return ((kv_state, offset + last_decay), (inside + carried, reach_decay))


def normalize(outputs):
    mean_square = jnp.mean(outputs * outputs, axis=-1, keepdims=True)
    return (outputs * lax.rsqrt(mean_square + 1e-06)).astype(jnp.bfloat16)


def relayed(devices):
    return devices == 8


def exchange_kernel(
    devices,
    capacity,
    own_ref,
    weight_hbm,
    slot_ref,
    flag_ref,
    direction_ref,
    out_ref,
    weight,
    blocks,
    total,
    tiles,
    landed,
    directions,
    weight_sem,
    block_send,
    block_recv,
    tile_send,
    tile_recv,
    direction_send,
    direction_recv,
):
    me = lax.axis_index("ep")
    core = lax.rem(me, 2)
    sibling = me + 1 - 2 * core
    rows, width = own_ref.shape
    half = rows // 2
    cols = weight.shape[0]
    pairs = devices // 2

    load = pltpu.make_async_copy(weight_hbm, weight, weight_sem)
    load.start()
    barrier = pltpu.get_barrier_semaphore()

    def greet(step, carry):
        pl.semaphore_signal(
            barrier, inc=1, device_id={"ep": lax.rem(me + step, devices)}, device_id_type=MESH
        )
        return carry

    lax.fori_loop(1, devices, greet, 0)
    pl.semaphore_wait(barrier, devices - 1)

    sends = []

    def part(ref, side):
        return ref.at[pl.ds(side * half, half)]

    def send(source, origin, side, target):
        copy = pltpu.make_async_remote_copy(
            src_ref=source,
            dst_ref=part(blocks.at[origin], side),
            send_sem=block_send.at[len(sends)],
            recv_sem=block_recv.at[origin, side],
            device_id={"ep": target},
            device_id_type=MESH,
        )
        copy.start()
        sends.append(copy)

    def arrived(origin, side):
        landing = part(blocks.at[origin], side)
        pltpu.make_async_copy(landing, landing, block_recv.at[origin, side]).wait()

    def forward(origin, side, target):
        send(part(blocks.at[origin], side), origin, side, target)

    def multiply(origin):
        columns = pl.ds(pl.multiple_of(origin * width, width), width)
        total[...] += lax.dot_general(
            blocks[origin],
            weight[:, columns],
            (((1,), (1,)), ((), ())),
            preferred_element_type=jnp.float32,
        )

    if relayed(devices):
        x_bit = lax.rem(me // 2, 2)
        y_bit = me // 4
        x_peer = me + 2 - 4 * x_bit
        y_peer = me + 4 - 8 * y_bit
        corner = x_peer + 4 - 8 * y_bit
        send(part(own_ref, 0), me, 0, x_peer)
        send(part(own_ref, 1), me, 1, y_peer)
        send(part(own_ref, 1), me, 1, x_peer)
        send(part(own_ref, 0), me, 0, y_peer)
    else:
        for step in range(1, pairs):
            peer = lax.rem(me + 2 * step, devices)
            for side in range(2):
                send(part(own_ref, side), me, side, peer)
    for side in range(2):
        send(part(own_ref, side), me, side, sibling)

    def share(step, carry):
        peer = lax.rem(me + step, devices)
        pltpu.make_async_remote_copy(
            src_ref=direction_ref,
            dst_ref=directions.at[me],
            send_sem=direction_send.at[step],
            recv_sem=direction_recv.at[me],
            device_id={"ep": peer},
            device_id_type=MESH,
        ).start()
        return carry

    lax.fori_loop(1, devices, share, 0)
    directions[pl.ds(me, 1)] = direction_ref[...][None]

    load.wait()
    columns = pl.ds(pl.multiple_of(me * width, width), width)
    total[...] = lax.dot_general(
        own_ref[...],
        weight[:, columns],
        (((1,), (1,)), ((), ())),
        preferred_element_type=jnp.float32,
    )

    if relayed(devices):
        arrived(x_peer, 0)
        forward(x_peer, 0, y_peer)
        forward(x_peer, 0, sibling)
        arrived(y_peer, 1)
        forward(y_peer, 1, x_peer)
        forward(y_peer, 1, sibling)
        arrived(x_peer, 1)
        forward(x_peer, 1, sibling)
        arrived(y_peer, 0)
        forward(y_peer, 0, sibling)
        arrived(sibling, 0)
        arrived(sibling, 1)

        def multiply_first(step, carry):
            origin = jnp.where(step == 0, sibling, jnp.where(step == 1, x_peer, y_peer))
            multiply(origin)
            return carry

        lax.fori_loop(0, 3, multiply_first, 0)
        arrived(corner, 0)
        forward(corner, 0, sibling)
        arrived(corner, 1)
        forward(corner, 1, sibling)
        multiply(corner)
        turn = sibling - me
        for origin in (x_peer, y_peer, corner):
            arrived(origin + turn, 0)
            arrived(origin + turn, 1)

        def multiply_last(step, carry):
            origin = jnp.where(step == 0, x_peer, jnp.where(step == 1, y_peer, corner))
            multiply(origin + turn)
            return carry

        lax.fori_loop(0, 3, multiply_last, 0)
    else:
        for step in range(1, pairs):
            origin = lax.rem(me + devices - 2 * step, devices)
            for side in range(2):
                arrived(origin, side)
                forward(origin, side, sibling)

        def multiply_same(step, carry):
            multiply(lax.rem(me + 2 * step, devices))
            return carry

        lax.fori_loop(1, pairs, multiply_same, 0)

        def multiply_other(step, carry):
            origin = lax.rem(sibling + 2 * step, devices)
            arrived(origin, 0)
            arrived(origin, 1)
            multiply(origin)
            return carry

        lax.fori_loop(0, pairs, multiply_other, 0)

    projected = total[...].astype(jnp.bfloat16)
    slots = lax.broadcasted_iota(jnp.int32, (capacity, rows), 0)

    def picked(expert):
        return slot_ref[expert] == slots

    def tile_of(expert):
        picks = jnp.where(picked(expert), 1.0, 0.0).astype(jnp.bfloat16)
        return jnp.dot(picks, projected, preferred_element_type=jnp.float32).astype(jnp.bfloat16)

    def tile_copy(expert):
        return pltpu.make_async_remote_copy(
            src_ref=tiles.at[expert],
            dst_ref=landed.at[me],
            send_sem=tile_send.at[expert],
            recv_sem=tile_recv.at[me],
            device_id={"ep": expert},
            device_id_type=MESH,
        )

    def dispatch(step, carry):
        expert = lax.rem(me + step, devices)
        tiles[expert] = tile_of(expert)
        tile_copy(expert).start()
        return carry

    lax.fori_loop(1, devices, dispatch, 0)
    landed[me] = tile_of(me)
    flags = jnp.sum(jnp.where(picked(me), flag_ref[...], 0.0), axis=1, keepdims=True) > 0.5

    def direction_wait(step, carry):
        origin = lax.rem(me + step, devices)
        landing = directions.at[origin]
        pltpu.make_async_copy(landing, landing, direction_recv.at[origin]).wait()
        return carry

    lax.fori_loop(1, devices, direction_wait, 0)
    squares = jnp.sum(directions[...] * directions[...], axis=0)
    norm_square = jnp.sum(squares, axis=1, keepdims=True) + 1e-06

    def product(origin):
        return jnp.sum(
            landed[origin].astype(jnp.float32) * directions[origin], axis=1, keepdims=True
        )

    def tile_wait(step, products):
        origin = lax.rem(me + step, devices)
        landing = landed.at[origin]
        pltpu.make_async_copy(landing, landing, tile_recv.at[origin]).wait()
        return products + product(origin)

    products = lax.fori_loop(1, devices, tile_wait, product(me))
    gain = products / norm_square

    def finish(origin, carry):
        tile = landed[origin]
        removed = (tile.astype(jnp.float32) - gain * directions[origin]).astype(jnp.bfloat16)
        result = jnp.where(flags, removed, tile)
        if cols % 128:
            out_ref[origin] = result
        else:
            out_ref[:, pl.ds(pl.multiple_of(origin * cols, cols), cols)] = result
        return carry

    lax.fori_loop(0, devices, finish, 0)

    for copy in sends:
        copy.wait_send()

    def sent(step, carry):
        expert = lax.rem(me + step, devices)
        tile_copy(expert).wait_send()
        pltpu.make_async_copy(direction_ref, direction_ref, direction_send.at[step]).wait()
        return carry

    lax.fori_loop(1, devices, sent, 0)


def project_and_dispatch(attended, out_weight, slot_index, row_flags, direction, capacity):
    devices = lax.axis_size("ep")
    rows, width = attended.shape
    cols = out_weight.shape[0]
    copies = 16 if relayed(devices) else 4 * devices
    shape = (devices, capacity, cols) if cols % 128 else (capacity, devices * cols)
    vmem = pl.BlockSpec(memory_space=pltpu.VMEM)
    return pl.pallas_call(
        functools.partial(exchange_kernel, devices, capacity),
        out_shape=jax.ShapeDtypeStruct(shape, jnp.bfloat16),
        in_specs=[vmem, pl.BlockSpec(memory_space=pl.ANY), vmem, vmem, vmem],
        out_specs=vmem,
        scratch_shapes=[
            pltpu.VMEM(out_weight.shape, jnp.bfloat16),
            pltpu.VMEM((devices, rows, width), jnp.bfloat16),
            pltpu.VMEM((rows, cols), jnp.float32),
            pltpu.VMEM((devices, capacity, cols), jnp.bfloat16),
            pltpu.VMEM((devices, capacity, cols), jnp.bfloat16),
            pltpu.VMEM((devices, 1, cols), jnp.float32),
            pltpu.SemaphoreType.DMA,
            pltpu.SemaphoreType.DMA((copies,)),
            pltpu.SemaphoreType.DMA((devices, 2)),
            pltpu.SemaphoreType.DMA((devices,)),
            pltpu.SemaphoreType.DMA((devices,)),
            pltpu.SemaphoreType.DMA((devices,)),
            pltpu.SemaphoreType.DMA((devices,)),
        ],
        compiler_params=pltpu.CompilerParams(
            collective_id=0, has_side_effects=True, vmem_limit_bytes=40 * 1024 * 1024
        ),
        cost_estimate=pl.CostEstimate(
            flops=2 * rows * devices * width * cols, bytes_accessed=out_weight.size * 2,
            transcendentals=0,
        ),
    )(attended, out_weight, slot_index, row_flags, direction)


def local(queries, key_rows, value_rows, log_decay, out_weight, expert_ids, flagged, direction):
    block_rows = queries.shape[0]
    local_width = queries.shape[1]
    local_heads = local_width // HEAD
    sub_count = block_rows // SUB
    model_cols = out_weight.shape[0]

    def shaped(operand):
        return operand.reshape(sub_count, SUB, local_heads, HEAD)

    start_state = (
        jnp.zeros((local_heads, HEAD, HEAD), jnp.float32),
        jnp.zeros((local_heads,), jnp.float32),
    )
    scanned = lax.scan(
        local_step,
        start_state,
        (
            shaped(queries),
            shaped(key_rows),
            shaped(value_rows),
            log_decay.reshape(sub_count, SUB, local_heads),
        ),
    )
    local_state, total_decay = scanned[0]
    partial_out, reach_decay = scanned[1]
    block_gain = jnp.exp(total_decay)

    def pass_state(hop_index, incoming):
        passed = block_gain[:, None, None] * incoming + local_state
        return passed_along(passed.astype(jnp.bfloat16), "ctx", 1).astype(jnp.float32)

    incoming = lax.fori_loop(0, lax.axis_size("ctx") - 1, pass_state, jnp.zeros_like(local_state))
    scaled = shaped(queries).astype(jnp.float32) * reach_decay[..., None]
    outputs = partial_out + jnp.einsum(
        "cthd,hde->cthe", scaled, incoming, precision=lax.Precision.HIGHEST
    )
    attended = normalize(outputs).reshape(block_rows, local_width)
    ctx_start = lax.axis_index("ctx") * block_rows
    local_flags = flagged - ctx_start
    experts_all = lax.axis_size("ep") * EXP_DEV
    capacity = 2 * block_rows * TOP // experts_all
    row_number = jnp.arange(block_rows, dtype=jnp.int32)
    expert_number = jnp.arange(experts_all, dtype=jnp.int32)
    named = jnp.any(expert_ids[:, :, None] == expert_number[None, None, :], axis=1)
    before = (row_number[:, None] > row_number[None, :]).astype(jnp.bfloat16)
    slot_index = jnp.dot(before, named.astype(jnp.bfloat16), preferred_element_type=jnp.float32)
    slot_index = jnp.where(named, slot_index.astype(jnp.int32), -1).T[:, None, :]
    row_flags = jnp.any(local_flags[:, None] == row_number[None, :], axis=0, keepdims=True)
    tiles = project_and_dispatch(
        attended,
        out_weight,
        slot_index,
        row_flags.astype(jnp.float32),
        direction[None, :],
        capacity,
    )
    if tiles.ndim == 3:
        tiles = jnp.transpose(tiles, (1, 0, 2)).reshape(capacity, -1)
    return tiles[None]


def solution(mesh):
    placed = (
        P("ctx", "ep"),
        P("ctx", "ep"),
        P("ctx", "ep"),
        P("ctx", "ep"),
        P("ep", None),
        P("ctx", None),
        P("ctx"),
        P("ep"),
    )
    return jax.shard_map(
        local, mesh=mesh, in_specs=placed, out_specs=P("ep", "ctx", None), check_vma=False
    )
```

```python
import functools

import jax
import jax.numpy as jnp
from jax import lax
from jax.experimental import pallas as pl
from jax.experimental.pallas import tpu as pltpu
from jax.sharding import PartitionSpec as P

HEAD = 128
TOP = 2
EXP_DEV = 1
SUB = 256
MESH = pl.DeviceIdType.MESH


def relayed(devices):
    return devices == 8


def layer_kernel(
    devices,
    blocks_of_sequence,
    capacity,
    query_ref,
    key_ref,
    value_ref,
    decay_ref,
    weight_hbm,
    slot_ref,
    flag_ref,
    direction_ref,
    out_ref,
    weight,
    cumulated,
    cumulated_rows,
    incoming,
    outgoing,
    attended,
    gathered,
    total,
    projected,
    spread_out,
    tiles,
    products,
    directions,
    weight_sem,
    state_send,
    state_recv,
    block_send,
    block_recv,
    row_send,
    row_recv,
    direction_send,
    direction_recv,
):
    me = lax.axis_index("ep")
    place = lax.axis_index("ctx")
    core = lax.rem(me, 2)
    turn = 1 - 2 * core
    sibling = me + turn
    rows, width = query_ref.shape
    heads = width // HEAD
    cols = weight.shape[0]
    pairs = devices // 2
    has_next = place < blocks_of_sequence - 1

    load = pltpu.make_async_copy(weight_hbm, weight, weight_sem)
    load.start()
    barrier = pltpu.get_barrier_semaphore()

    def greet(step, carry):
        pl.semaphore_signal(
            barrier, inc=1, device_id={"ep": lax.rem(me + step, devices)}, device_id_type=MESH
        )
        return carry

    lax.fori_loop(1, devices, greet, 0)

    @pl.when(place > 0)
    def _():
        pl.semaphore_signal(barrier, inc=1, device_id={"ctx": place - 1}, device_id_type=MESH)

    t_index = lax.broadcasted_iota(jnp.int32, (rows, rows), 0)
    s_index = lax.broadcasted_iota(jnp.int32, (rows, rows), 1)
    causal = t_index >= s_index
    lower = jnp.where(causal, 1.0, 0.0)
    cumulated[...] = jnp.dot(
        lower,
        decay_ref[...],
        precision=lax.Precision.HIGHEST,
        preferred_element_type=jnp.float32,
    )
    whole_rows = jnp.transpose(cumulated[...])
    for head in range(heads):
        cumulated_rows[head] = whole_rows[head : head + 1, :]

    pl.semaphore_wait(barrier, devices - 1 + jnp.where(has_next, 1, 0))

    def share(step, carry):
        pltpu.make_async_remote_copy(
            src_ref=direction_ref,
            dst_ref=directions.at[me],
            send_sem=direction_send.at[step],
            recv_sem=direction_recv.at[me],
            device_id={"ep": lax.rem(me + step, devices)},
            device_id_type=MESH,
        ).start()
        return carry

    lax.fori_loop(1, devices, share, 0)
    directions[pl.ds(me, 1)] = direction_ref[...][None]

    def state_copy(head):
        return pltpu.make_async_remote_copy(
            src_ref=outgoing.at[head],
            dst_ref=incoming.at[head],
            send_sem=state_send.at[head],
            recv_sem=state_recv.at[head],
            device_id={"ctx": place + 1},
            device_id_type=MESH,
        )

    head_lane = lax.broadcasted_iota(jnp.int32, (rows, heads), 1)

    def attend(side, step, carry):
        head = side * (heads // 2) + step
        columns = pl.ds(pl.multiple_of(head * HEAD, HEAD), HEAD)
        query, key, value = query_ref[:, columns], key_ref[:, columns], value_ref[:, columns]
        level = jnp.sum(
            jnp.where(head_lane == head, cumulated[...], 0.0), axis=1, keepdims=True
        )
        last = level[rows - 1 :, :]
        key_scaled = (key.astype(jnp.float32) * jnp.exp(last - level)).astype(jnp.bfloat16)
        state = lax.dot_general(
            key_scaled, value, (((0,), (0,)), ((), ())), preferred_element_type=jnp.float32
        )
        scores = lax.dot_general(
            query, key, (((1,), (1,)), ((), ())), preferred_element_type=jnp.float32
        )
        gaps = jnp.minimum(level - cumulated_rows[head], 0.0)
        weights = jnp.where(causal, scores * jnp.exp(gaps), 0.0).astype(jnp.bfloat16)
        inside = jnp.dot(weights, value, preferred_element_type=jnp.float32)

        @pl.when(place == 0)
        def _():
            incoming[head] = jnp.zeros((HEAD, HEAD), jnp.bfloat16)

        @pl.when(place > 0)
        def _():
            landing = incoming.at[head]
            pltpu.make_async_copy(landing, landing, state_recv.at[head]).wait()

        before = incoming[head]

        @pl.when(has_next)
        def _():
            outgoing[head] = (jnp.exp(last) * before.astype(jnp.float32) + state).astype(
                jnp.bfloat16
            )
            state_copy(head).start()

        carried = jnp.dot(query, before, preferred_element_type=jnp.float32)
        outputs = inside + jnp.exp(level) * carried
        mean_square = jnp.mean(outputs * outputs, axis=1, keepdims=True)
        own = pl.ds(pl.multiple_of(step * HEAD, HEAD), HEAD)
        attended[side, :, own] = (outputs * lax.rsqrt(mean_square + 1e-06)).astype(jnp.bfloat16)
        return carry

    sends = []
    if relayed(devices):
        x_peer = me + 2 - 4 * lax.rem(me // 2, 2)
        y_peer = me + 4 - 8 * (me // 4)
        corner = x_peer + y_peer - me

    def exchange(own, buffer, send_sem, recv_sem):
        count = []

        def send(source, origin, side, target):
            copy = pltpu.make_async_remote_copy(
                src_ref=source,
                dst_ref=buffer.at[origin, side],
                send_sem=send_sem.at[len(count)],
                recv_sem=recv_sem.at[origin, side],
                device_id={"ep": target},
                device_id_type=MESH,
            )
            copy.start()
            count.append(copy)
            sends.append(copy)

        def arrived(origin, side):
            landing = buffer.at[origin, side]
            pltpu.make_async_copy(landing, landing, recv_sem.at[origin, side]).wait()

        def forward(origin, side, target):
            send(buffer.at[origin, side], origin, side, target)

        def begin(side):
            if relayed(devices):
                peers = (x_peer, y_peer) if side == 0 else (y_peer, x_peer)
            else:
                peers = [lax.rem(me + 2 * step, devices) for step in range(1, pairs)]
            for peer in peers:
                send(own.at[side], me, side, peer)
            send(own.at[side], me, side, sibling)

        def take(use):
            if relayed(devices):
                arrived(x_peer, 0)
                forward(x_peer, 0, y_peer)
                forward(x_peer, 0, sibling)
                arrived(y_peer, 0)
                forward(y_peer, 0, sibling)
                arrived(y_peer, 1)
                forward(y_peer, 1, x_peer)
                forward(y_peer, 1, sibling)
                arrived(x_peer, 1)
                forward(x_peer, 1, sibling)
                arrived(sibling, 0)
                arrived(sibling, 1)

                def use_first(step, carry):
                    use(jnp.where(step == 0, sibling, jnp.where(step == 1, x_peer, y_peer)))
                    return carry

                lax.fori_loop(0, 3, use_first, 0)
                for origin in (x_peer, y_peer):
                    arrived(origin + turn, 0)
                    arrived(origin + turn, 1)

                def use_second(step, carry):
                    use(jnp.where(step == 0, x_peer, y_peer) + turn)
                    return carry

                arrived(corner, 0)
                forward(corner, 0, sibling)
                lax.fori_loop(0, 2, use_second, 0)
                arrived(corner, 1)
                forward(corner, 1, sibling)

                def use_last(step, carry):
                    origin = corner + turn * step
                    for side in range(2):
                        @pl.when(step == 1)
                        def _():
                            arrived(origin, side)
                    use(origin)
                    return carry

                lax.fori_loop(0, 2, use_last, 0)
            else:
                for step in range(1, pairs):
                    origin = lax.rem(me + devices - 2 * step, devices)
                    for side in range(2):
                        arrived(origin, side)
                        forward(origin, side, sibling)

                def use_same(step, carry):
                    use(lax.rem(me + 2 * step, devices))
                    return carry

                lax.fori_loop(1, pairs, use_same, 0)

                def use_other(step, carry):
                    origin = lax.rem(sibling + 2 * step, devices)
                    arrived(origin, 0)
                    arrived(origin, 1)
                    use(origin)
                    return carry

                lax.fori_loop(0, pairs, use_other, 0)

        return begin, take

    begin, take = exchange(attended, gathered, block_send, block_recv)
    for side in range(2):
        lax.fori_loop(0, heads // 2, functools.partial(attend, side), 0)
        begin(side)

    half = width // 2

    def multiplied(block, origin):
        result = None
        for side in range(2):
            columns = pl.ds(pl.multiple_of(origin * width + side * half, half), half)
            term = lax.dot_general(
                block[side],
                weight[:, columns],
                (((1,), (1,)), ((), ())),
                preferred_element_type=jnp.float32,
            )
            result = term if result is None else result + term
        return result

    load.wait()
    total[...] = multiplied(attended, me)

    def multiply(origin):
        total[...] += multiplied(gathered.at[origin], origin)

    take(multiply)

    begin, take = exchange(projected, spread_out, row_send, row_recv)
    part = rows // 2
    for side in range(2):
        projected[side] = total[side * part : (side + 1) * part, :].astype(jnp.bfloat16)
        begin(side)

    slots = lax.broadcasted_iota(jnp.int32, (capacity, rows), 0)
    picked = slot_ref[me] == slots
    picks = jnp.where(picked, 1.0, 0.0).astype(jnp.bfloat16)
    flags = jnp.sum(jnp.where(picked, flag_ref[...], 0.0), axis=1, keepdims=True) > 0.5

    def direction_wait(step, carry):
        origin = lax.rem(me + step, devices)
        landing = directions.at[origin]
        pltpu.make_async_copy(landing, landing, direction_recv.at[origin]).wait()
        return carry

    lax.fori_loop(1, devices, direction_wait, 0)
    squares = jnp.sum(directions[...] * directions[...], axis=0)
    norm_square = jnp.sum(squares, axis=1, keepdims=True) + 1e-06

    def pick(block, origin):
        picked_rows = jnp.dot(
            picks[:, :part], block[0], preferred_element_type=jnp.float32
        ) + jnp.dot(picks[:, part:], block[1], preferred_element_type=jnp.float32)
        tiles[origin] = picked_rows.astype(jnp.bfloat16)
        return jnp.sum(picked_rows * directions[origin], axis=1, keepdims=True)

    products[...] = pick(projected, me)

    def collect(origin):
        products[...] += pick(spread_out.at[origin], origin)

    take(collect)
    gain = products[...] / norm_square

    def finish(origin, carry):
        tile = tiles[origin]
        removed = (tile.astype(jnp.float32) - gain * directions[origin]).astype(jnp.bfloat16)
        result = jnp.where(flags, removed, tile)
        if cols % 128:
            out_ref[origin] = result
        else:
            out_ref[:, pl.ds(pl.multiple_of(origin * cols, cols), cols)] = result
        return carry

    lax.fori_loop(0, devices, finish, 0)

    for copy in sends:
        copy.wait_send()

    @pl.when(has_next)
    def _():
        def state_sent(head, carry):
            state_copy(head).wait_send()
            return carry

        lax.fori_loop(0, heads, state_sent, 0)

    def sent(step, carry):
        pltpu.make_async_copy(direction_ref, direction_ref, direction_send.at[step]).wait()
        return carry

    lax.fori_loop(1, devices, sent, 0)


def layer(
    queries, key_rows, value_rows, log_decay, out_weight, slot_index, row_flags, direction, capacity
):
    devices = lax.axis_size("ep")
    rows, width = queries.shape
    heads = width // HEAD
    cols = out_weight.shape[0]
    copies = 16 if relayed(devices) else 2 * devices
    shape = (devices, capacity, cols) if cols % 128 else (capacity, devices * cols)
    vmem = pl.BlockSpec(memory_space=pltpu.VMEM)
    dma = pltpu.SemaphoreType.DMA
    return pl.pallas_call(
        functools.partial(layer_kernel, devices, lax.axis_size("ctx"), capacity),
        out_shape=jax.ShapeDtypeStruct(shape, jnp.bfloat16),
        in_specs=[vmem] * 4 + [pl.BlockSpec(memory_space=pl.ANY)] + [vmem] * 3,
        out_specs=vmem,
        scratch_shapes=[
            pltpu.VMEM(out_weight.shape, jnp.bfloat16),
            pltpu.VMEM((rows, heads), jnp.float32),
            pltpu.VMEM((heads, 1, rows), jnp.float32),
            pltpu.VMEM((heads, HEAD, HEAD), jnp.bfloat16),
            pltpu.VMEM((heads, HEAD, HEAD), jnp.bfloat16),
            pltpu.VMEM((2, rows, width // 2), jnp.bfloat16),
            pltpu.VMEM((devices, 2, rows, width // 2), jnp.bfloat16),
            pltpu.VMEM((rows, cols), jnp.float32),
            pltpu.VMEM((2, rows // 2, cols), jnp.bfloat16),
            pltpu.VMEM((devices, 2, rows // 2, cols), jnp.bfloat16),
            pltpu.VMEM((devices, capacity, cols), jnp.bfloat16),
            pltpu.VMEM((capacity, 1), jnp.float32),
            pltpu.VMEM((devices, 1, cols), jnp.float32),
            dma,
            dma((heads,)),
            dma((heads,)),
            dma((copies,)),
            dma((devices, 2)),
            dma((copies,)),
            dma((devices, 2)),
            dma((devices,)),
            dma((devices,)),
        ],
        compiler_params=pltpu.CompilerParams(
            collective_id=0, has_side_effects=True, vmem_limit_bytes=44 * 1024 * 1024
        ),
        cost_estimate=pl.CostEstimate(
            flops=2 * rows * devices * width * cols, bytes_accessed=out_weight.size * 2,
            transcendentals=0,
        ),
    )(queries, key_rows, value_rows, log_decay, out_weight, slot_index, row_flags, direction)


def local(queries, key_rows, value_rows, log_decay, out_weight, expert_ids, flagged, direction):
    block_rows = queries.shape[0]
    assert block_rows == SUB
    ctx_start = lax.axis_index("ctx") * block_rows
    local_flags = flagged - ctx_start
    experts_all = lax.axis_size("ep") * EXP_DEV
    capacity = 2 * block_rows * TOP // experts_all
    row_number = jnp.arange(block_rows, dtype=jnp.int32)
    expert_number = jnp.arange(experts_all, dtype=jnp.int32)
    named = jnp.any(expert_ids[:, :, None] == expert_number[None, None, :], axis=1)
    before = (row_number[:, None] > row_number[None, :]).astype(jnp.bfloat16)
    slot_index = jnp.dot(before, named.astype(jnp.bfloat16), preferred_element_type=jnp.float32)
    slot_index = jnp.where(named, slot_index.astype(jnp.int32), -1).T[:, None, :]
    row_flags = jnp.any(local_flags[:, None] == row_number[None, :], axis=0, keepdims=True)
    tiles = layer(
        queries,
        key_rows,
        value_rows,
        log_decay,
        out_weight,
        slot_index,
        row_flags.astype(jnp.float32),
        direction[None, :],
        capacity,
    )
    if tiles.ndim == 3:
        tiles = jnp.transpose(tiles, (1, 0, 2)).reshape(capacity, -1)
    return tiles[None]


def solution(mesh):
    placed = (
        P("ctx", "ep"),
        P("ctx", "ep"),
        P("ctx", "ep"),
        P("ctx", "ep"),
        P("ep", None),
        P("ctx", None),
        P("ctx"),
        P("ep"),
    )
    return jax.shard_map(
        local, mesh=mesh, in_specs=placed, out_specs=P("ep", "ctx", None), check_vma=False
    )
```

```python
import functools

import jax
import jax.numpy as jnp
from jax import lax
from jax.experimental import pallas as pl
from jax.experimental.pallas import tpu as pltpu
from jax.sharding import PartitionSpec as P

HEAD = 128
TOP = 2
EXP_DEV = 1
SUB = 256
MESH = pl.DeviceIdType.MESH


def relayed(devices):
    return devices == 8


def layer_kernel(
    devices,
    blocks_of_sequence,
    capacity,
    query_hbm,
    key_hbm,
    value_hbm,
    decay_ref,
    weight_hbm,
    named_ref,
    flagged_ref,
    direction_ref,
    out_ref,
    weight,
    heads_in,
    inside,
    growth,
    states,
    cumulated,
    cumulated_rows,
    incoming,
    outgoing,
    attended,
    gathered,
    total,
    projected,
    spread_out,
    tiles,
    products,
    directions,
    weight_sem,
    heads_sem,
    state_send,
    state_recv,
    block_send,
    block_recv,
    row_send,
    row_recv,
    direction_send,
    direction_recv,
):
    me = lax.axis_index("ep")
    place = lax.axis_index("ctx")
    core = lax.rem(me, 2)
    turn = 1 - 2 * core
    sibling = me + turn
    rows, width = query_hbm.shape
    half = width // 2
    heads = width // HEAD
    cols = weight.shape[0]
    pairs = devices // 2
    has_next = place < blocks_of_sequence - 1

    def heads_copy(side, which):
        source = (query_hbm, key_hbm, value_hbm)[which]
        return pltpu.make_async_copy(
            source.at[:, pl.ds(side * half, half)],
            heads_in.at[side, which],
            heads_sem.at[side, which],
        )

    for side in range(2):
        for which in range(3):
            heads_copy(side, which).start()
    load = pltpu.make_async_copy(weight_hbm, weight, weight_sem)
    load.start()
    barrier = pltpu.get_barrier_semaphore()

    def greet(step, carry):
        pl.semaphore_signal(
            barrier, inc=1, device_id={"ep": lax.rem(me + step, devices)}, device_id_type=MESH
        )
        return carry

    lax.fori_loop(1, devices, greet, 0)

    @pl.when(place > 0)
    def _():
        pl.semaphore_signal(barrier, inc=1, device_id={"ctx": place - 1}, device_id_type=MESH)

    t_index = lax.broadcasted_iota(jnp.int32, (rows, rows), 0)
    s_index = lax.broadcasted_iota(jnp.int32, (rows, rows), 1)
    causal = t_index >= s_index
    upper = jnp.where(t_index <= s_index, 1.0, 0.0)
    whole_rows = jnp.dot(
        decay_ref[...],
        upper,
        precision=lax.Precision.HIGHEST,
        preferred_element_type=jnp.float32,
    )
    cumulated[...] = jnp.transpose(whole_rows)
    for head in range(heads):
        cumulated_rows[head] = whole_rows[head : head + 1, :]

    pl.semaphore_wait(barrier, devices - 1 + jnp.where(has_next, 1, 0))

    def share(step, carry):
        pltpu.make_async_remote_copy(
            src_ref=direction_ref,
            dst_ref=directions.at[me],
            send_sem=direction_send.at[step],
            recv_sem=direction_recv.at[me],
            device_id={"ep": lax.rem(me + step, devices)},
            device_id_type=MESH,
        ).start()
        return carry

    lax.fori_loop(1, devices, share, 0)
    directions[pl.ds(me, 1)] = direction_ref[...][None]

    def state_copy(head):
        return pltpu.make_async_remote_copy(
            src_ref=outgoing.at[head],
            dst_ref=incoming.at[head],
            send_sem=state_send.at[head],
            recv_sem=state_recv.at[head],
            device_id={"ctx": place + 1},
            device_id_type=MESH,
        )

    head_lane = lax.broadcasted_iota(jnp.int32, (rows, heads), 1)

    def within(side, step, carry):
        head = side * (heads // 2) + step
        columns = pl.ds(pl.multiple_of(step * HEAD, HEAD), HEAD)
        query, key, value = (heads_in[side, which, :, columns] for which in range(3))
        level = jnp.sum(
            jnp.where(head_lane == head, cumulated[...], 0.0), axis=1, keepdims=True
        )
        last = level[rows - 1 :, :]
        key_scaled = (key.astype(jnp.float32) * jnp.exp(last - level)).astype(jnp.bfloat16)
        states[head] = lax.dot_general(
            key_scaled, value, (((0,), (0,)), ((), ())), preferred_element_type=jnp.float32
        )
        scores = lax.dot_general(
            query, key, (((1,), (1,)), ((), ())), preferred_element_type=jnp.float32
        )
        gaps = jnp.minimum(level - cumulated_rows[head], 0.0)
        weights = jnp.where(causal, scores * jnp.exp(gaps), 0.0).astype(jnp.bfloat16)
        inside[head] = jnp.dot(weights, value, preferred_element_type=jnp.float32)
        growth[head] = jnp.exp(level)
        return carry

    def pass_on(side, step, carry):
        head = side * (heads // 2) + step

        @pl.when(place > 0)
        def _():
            landing = incoming.at[head]
            pltpu.make_async_copy(landing, landing, state_recv.at[head]).wait()

        @pl.when(has_next)
        def _():
            gain = growth[head, rows - 1 :, :]
            outgoing[head] = (gain * incoming[head].astype(jnp.float32) + states[head]).astype(
                jnp.bfloat16
            )
            state_copy(head).start()

        return carry

    def across(side, step, carry):
        head = side * (heads // 2) + step
        columns = pl.ds(pl.multiple_of(step * HEAD, HEAD), HEAD)
        carried = jnp.dot(
            heads_in[side, 0, :, columns], incoming[head], preferred_element_type=jnp.float32
        )
        outputs = inside[head] + growth[head] * carried
        mean_square = jnp.mean(outputs * outputs, axis=1, keepdims=True)
        attended[side, :, columns] = (outputs * lax.rsqrt(mean_square + 1e-06)).astype(
            jnp.bfloat16
        )
        return carry

    @pl.when(place == 0)
    def _():
        incoming[...] = jnp.zeros(incoming.shape, incoming.dtype)

    sends = []
    if relayed(devices):
        x_peer = me + 2 - 4 * lax.rem(me // 2, 2)
        y_peer = me + 4 - 8 * (me // 4)
        corner = x_peer + y_peer - me

    def exchange(own, buffer, send_sem, recv_sem):
        count = []

        def send(source, origin, side, target):
            copy = pltpu.make_async_remote_copy(
                src_ref=source,
                dst_ref=buffer.at[origin, side],
                send_sem=send_sem.at[len(count)],
                recv_sem=recv_sem.at[origin, side],
                device_id={"ep": target},
                device_id_type=MESH,
            )
            copy.start()
            count.append(copy)
            sends.append(copy)

        def arrived(origin, side):
            landing = buffer.at[origin, side]
            pltpu.make_async_copy(landing, landing, recv_sem.at[origin, side]).wait()

        def forward(origin, side, target):
            send(buffer.at[origin, side], origin, side, target)

        def begin(side):
            if relayed(devices):
                peers = (x_peer, y_peer) if side == 0 else (y_peer, x_peer)
            else:
                peers = [lax.rem(me + 2 * step, devices) for step in range(1, pairs)]
            for peer in peers:
                send(own.at[side], me, side, peer)
            send(own.at[side], me, side, sibling)

        def take(use):
            if relayed(devices):
                arrived(x_peer, 0)
                forward(x_peer, 0, y_peer)
                forward(x_peer, 0, sibling)
                arrived(y_peer, 0)
                forward(y_peer, 0, sibling)
                arrived(y_peer, 1)
                forward(y_peer, 1, x_peer)
                forward(y_peer, 1, sibling)
                arrived(x_peer, 1)
                forward(x_peer, 1, sibling)
                arrived(sibling, 0)
                arrived(sibling, 1)

                def use_first(step, carry):
                    use(jnp.where(step == 0, sibling, jnp.where(step == 1, x_peer, y_peer)))
                    return carry

                lax.fori_loop(0, 3, use_first, 0)
                for origin in (x_peer, y_peer):
                    arrived(origin + turn, 0)
                    arrived(origin + turn, 1)

                def use_second(step, carry):
                    use(jnp.where(step == 0, x_peer, y_peer) + turn)
                    return carry

                arrived(corner, 0)
                forward(corner, 0, sibling)
                lax.fori_loop(0, 2, use_second, 0)
                arrived(corner, 1)
                forward(corner, 1, sibling)

                def use_last(step, carry):
                    origin = corner + turn * step
                    for side in range(2):
                        @pl.when(step == 1)
                        def _():
                            arrived(origin, side)
                    use(origin)
                    return carry

                lax.fori_loop(0, 2, use_last, 0)
            else:
                for step in range(1, pairs):
                    origin = lax.rem(me + devices - 2 * step, devices)
                    for side in range(2):
                        arrived(origin, side)
                        forward(origin, side, sibling)

                def use_same(step, carry):
                    use(lax.rem(me + 2 * step, devices))
                    return carry

                lax.fori_loop(1, pairs, use_same, 0)

                def use_other(step, carry):
                    origin = lax.rem(sibling + 2 * step, devices)
                    arrived(origin, 0)
                    arrived(origin, 1)
                    use(origin)
                    return carry

                lax.fori_loop(0, pairs, use_other, 0)

        return begin, take

    begin, take = exchange(attended, gathered, block_send, block_recv)
    for side in range(2):
        for which in range(3):
            heads_copy(side, which).wait()
        count = heads // 2
        lax.fori_loop(0, count, functools.partial(within, side), 0, unroll=True)
        lax.fori_loop(0, count, functools.partial(pass_on, side), 0)
        lax.fori_loop(0, count, functools.partial(across, side), 0, unroll=True)
        begin(side)

    def multiplied(block, origin):
        result = None
        for side in range(2):
            columns = pl.ds(pl.multiple_of(origin * width + side * half, half), half)
            term = lax.dot_general(
                block[side],
                weight[:, columns],
                (((1,), (1,)), ((), ())),
                preferred_element_type=jnp.float32,
            )
            result = term if result is None else result + term
        return result

    load.wait()
    total[...] = multiplied(attended, me)

    def multiply(origin):
        total[...] += multiplied(gathered.at[origin], origin)

    take(multiply)

    begin, take = exchange(projected, spread_out, row_send, row_recv)
    part = rows // 2
    for side in range(2):
        projected[side] = total[side * part : (side + 1) * part, :].astype(jnp.bfloat16)
        begin(side)

    slots = lax.broadcasted_iota(jnp.int32, (capacity, rows), 0)
    named = jnp.max(jnp.where(named_ref[...] == me, 1.0, 0.0), axis=0, keepdims=True)
    earlier = jnp.where(t_index < s_index, 1.0, 0.0).astype(jnp.bfloat16)
    slot = jnp.dot(
        jnp.broadcast_to(named, (16, rows)).astype(jnp.bfloat16),
        earlier,
        preferred_element_type=jnp.float32,
    )[0:1, :]
    slot = jnp.where(named > 0.5, slot, -1.0).astype(jnp.int32)
    picked = slot == slots
    picks = jnp.where(picked, 1.0, 0.0).astype(jnp.bfloat16)
    row_number = lax.broadcasted_iota(jnp.int32, (1, rows), 1) + place * rows

    def flag(index, flags):
        return jnp.where(row_number == flagged_ref[index], 1.0, flags)

    row_flags = lax.fori_loop(
        0, flagged_ref.shape[0], flag, jnp.zeros((1, rows), jnp.float32), unroll=8
    )
    flags = jnp.sum(jnp.where(picked, row_flags, 0.0), axis=1, keepdims=True) > 0.5

    def direction_wait(step, carry):
        origin = lax.rem(me + step, devices)
        landing = directions.at[origin]
        pltpu.make_async_copy(landing, landing, direction_recv.at[origin]).wait()
        return carry

    lax.fori_loop(1, devices, direction_wait, 0)
    squares = jnp.sum(directions[...] * directions[...], axis=0)
    norm_square = jnp.sum(squares, axis=1, keepdims=True) + 1e-06

    def pick(block, origin):
        picked_rows = jnp.dot(
            picks[:, :part], block[0], preferred_element_type=jnp.float32
        ) + jnp.dot(picks[:, part:], block[1], preferred_element_type=jnp.float32)
        tiles[origin] = picked_rows.astype(jnp.bfloat16)
        return jnp.sum(picked_rows * directions[origin], axis=1, keepdims=True)

    products[...] = pick(projected, me)

    def collect(origin):
        products[...] += pick(spread_out.at[origin], origin)

    take(collect)
    gain = products[...] / norm_square

    def finish(origin, carry):
        tile = tiles[origin]
        removed = (tile.astype(jnp.float32) - gain * directions[origin]).astype(jnp.bfloat16)
        result = jnp.where(flags, removed, tile)
        if cols % 128:
            out_ref[origin] = result
        else:
            out_ref[:, pl.ds(pl.multiple_of(origin * cols, cols), cols)] = result
        return carry

    lax.fori_loop(0, devices, finish, 0)

    for copy in sends:
        copy.wait_send()

    @pl.when(has_next)
    def _():
        def state_sent(head, carry):
            state_copy(head).wait_send()
            return carry

        lax.fori_loop(0, heads, state_sent, 0)

    def sent(step, carry):
        pltpu.make_async_copy(direction_ref, direction_ref, direction_send.at[step]).wait()
        return carry

    lax.fori_loop(1, devices, sent, 0)


def layer(
    queries, key_rows, value_rows, decay, out_weight, named, flagged, direction, capacity
):
    devices = lax.axis_size("ep")
    rows, width = queries.shape
    heads = width // HEAD
    cols = out_weight.shape[0]
    copies = 16 if relayed(devices) else 2 * devices
    shape = (devices, capacity, cols) if cols % 128 else (capacity, devices * cols)
    vmem = pl.BlockSpec(memory_space=pltpu.VMEM)
    hbm = pl.BlockSpec(memory_space=pl.ANY)
    dma = pltpu.SemaphoreType.DMA
    return pl.pallas_call(
        functools.partial(layer_kernel, devices, lax.axis_size("ctx"), capacity),
        out_shape=jax.ShapeDtypeStruct(shape, jnp.bfloat16),
        in_specs=[hbm] * 3 + [vmem, hbm, vmem, pl.BlockSpec(memory_space=pltpu.SMEM), vmem],
        out_specs=vmem,
        scratch_shapes=[
            pltpu.VMEM(out_weight.shape, jnp.bfloat16),
            pltpu.VMEM((2, 3, rows, width // 2), jnp.bfloat16),
            pltpu.VMEM((heads, rows, HEAD), jnp.float32),
            pltpu.VMEM((heads, rows, 1), jnp.float32),
            pltpu.VMEM((heads, HEAD, HEAD), jnp.float32),
            pltpu.VMEM((rows, heads), jnp.float32),
            pltpu.VMEM((heads, 1, rows), jnp.float32),
            pltpu.VMEM((heads, HEAD, HEAD), jnp.bfloat16),
            pltpu.VMEM((heads, HEAD, HEAD), jnp.bfloat16),
            pltpu.VMEM((2, rows, width // 2), jnp.bfloat16),
            pltpu.VMEM((devices, 2, rows, width // 2), jnp.bfloat16),
            pltpu.VMEM((rows, cols), jnp.float32),
            pltpu.VMEM((2, rows // 2, cols), jnp.bfloat16),
            pltpu.VMEM((devices, 2, rows // 2, cols), jnp.bfloat16),
            pltpu.VMEM((devices, capacity, cols), jnp.bfloat16),
            pltpu.VMEM((capacity, 1), jnp.float32),
            pltpu.VMEM((devices, 1, cols), jnp.float32),
            dma,
            dma((2, 3)),
            dma((heads,)),
            dma((heads,)),
            dma((copies,)),
            dma((devices, 2)),
            dma((copies,)),
            dma((devices, 2)),
            dma((devices,)),
            dma((devices,)),
        ],
        compiler_params=pltpu.CompilerParams(
            collective_id=0, has_side_effects=True, vmem_limit_bytes=58 * 1024 * 1024
        ),
        cost_estimate=pl.CostEstimate(
            flops=2 * rows * devices * width * cols, bytes_accessed=out_weight.size * 2,
            transcendentals=0,
        ),
    )(queries, key_rows, value_rows, decay, out_weight, named, flagged, direction)


def local(queries, key_rows, value_rows, log_decay, out_weight, expert_ids, flagged, direction):
    block_rows = queries.shape[0]
    assert block_rows == SUB
    experts_all = lax.axis_size("ep") * EXP_DEV
    capacity = 2 * block_rows * TOP // experts_all
    tiles = layer(
        queries,
        key_rows,
        value_rows,
        log_decay.T,
        out_weight,
        expert_ids.T,
        flagged,
        direction[None, :],
        capacity,
    )
    if tiles.ndim == 3:
        tiles = jnp.transpose(tiles, (1, 0, 2)).reshape(capacity, -1)
    return tiles[None]


def solution(mesh):
    placed = (
        P("ctx", "ep"),
        P("ctx", "ep"),
        P("ctx", "ep"),
        P("ctx", "ep"),
        P("ep", None),
        P("ctx", None),
        P("ctx"),
        P("ep"),
    )
    return jax.shard_map(
        local, mesh=mesh, in_specs=placed, out_specs=P("ep", "ctx", None), check_vma=False
    )
```

```python
import functools

import jax
import jax.numpy as jnp
from jax import lax
from jax.experimental import pallas as pl
from jax.experimental.pallas import tpu as pltpu
from jax.sharding import PartitionSpec as P

HEAD = 128
TOP = 2
EXP_DEV = 1
SUB = 256
MESH = pl.DeviceIdType.MESH


def relayed(devices):
    return devices == 8


def layer_kernel(
    devices,
    blocks_of_sequence,
    capacity,
    query_hbm,
    key_hbm,
    value_hbm,
    decay_ref,
    weight_hbm,
    named_ref,
    flagged_ref,
    direction_ref,
    out_ref,
    weight,
    heads_in,
    inside,
    levels,
    growth,
    states,
    cumulated,
    cumulated_rows,
    incoming,
    outgoing,
    attended,
    gathered,
    total,
    projected,
    spread_out,
    tiles,
    products,
    directions,
    weight_sem,
    heads_sem,
    state_send,
    state_recv,
    block_send,
    block_recv,
    row_send,
    row_recv,
    direction_send,
    direction_recv,
):
    me = lax.axis_index("ep")
    place = lax.axis_index("ctx")
    core = lax.rem(me, 2)
    turn = 1 - 2 * core
    sibling = me + turn
    rows, width = query_hbm.shape
    half = width // 2
    heads = width // HEAD
    cols = weight.shape[0]
    pairs = devices // 2
    has_next = place < blocks_of_sequence - 1

    def heads_copy(side, which):
        source = (query_hbm, key_hbm, value_hbm)[which]
        return pltpu.make_async_copy(
            source.at[:, pl.ds(side * half, half)],
            heads_in.at[side, which],
            heads_sem.at[side, which],
        )

    for side in range(2):
        for which in range(3):
            heads_copy(side, which).start()
    load = pltpu.make_async_copy(weight_hbm, weight, weight_sem)
    load.start()
    barrier = pltpu.get_barrier_semaphore()

    def greet(step, carry):
        pl.semaphore_signal(
            barrier, inc=1, device_id={"ep": lax.rem(me + step, devices)}, device_id_type=MESH
        )
        return carry

    lax.fori_loop(1, devices, greet, 0)

    @pl.when(place > 0)
    def _():
        pl.semaphore_signal(barrier, inc=1, device_id={"ctx": place - 1}, device_id_type=MESH)

    t_index = lax.broadcasted_iota(jnp.int32, (rows, rows), 0)
    s_index = lax.broadcasted_iota(jnp.int32, (rows, rows), 1)
    causal = t_index >= s_index
    upper = jnp.where(t_index <= s_index, 1.0, 0.0)
    whole_rows = jnp.dot(
        decay_ref[...],
        upper,
        precision=lax.Precision.HIGHEST,
        preferred_element_type=jnp.float32,
    )
    cumulated[...] = jnp.transpose(whole_rows)
    for head in range(heads):
        cumulated_rows[head] = whole_rows[head : head + 1, :]

    pl.semaphore_wait(barrier, devices - 1 + jnp.where(has_next, 1, 0))

    def share(step, carry):
        pltpu.make_async_remote_copy(
            src_ref=direction_ref,
            dst_ref=directions.at[me],
            send_sem=direction_send.at[step],
            recv_sem=direction_recv.at[me],
            device_id={"ep": lax.rem(me + step, devices)},
            device_id_type=MESH,
        ).start()
        return carry

    lax.fori_loop(1, devices, share, 0)
    directions[pl.ds(me, 1)] = direction_ref[...][None]

    def state_copy(head):
        return pltpu.make_async_remote_copy(
            src_ref=outgoing.at[head],
            dst_ref=incoming.at[head],
            send_sem=state_send.at[head],
            recv_sem=state_recv.at[head],
            device_id={"ctx": place + 1},
            device_id_type=MESH,
        )

    head_lane = lax.broadcasted_iota(jnp.int32, (rows, heads), 1)

    def update(side, step, carry):
        head = side * (heads // 2) + step
        columns = pl.ds(pl.multiple_of(step * HEAD, HEAD), HEAD)
        key, value = heads_in[side, 1, :, columns], heads_in[side, 2, :, columns]
        level = jnp.sum(
            jnp.where(head_lane == head, cumulated[...], 0.0), axis=1, keepdims=True
        )
        last = level[rows - 1 :, :]
        key_scaled = (key.astype(jnp.float32) * jnp.exp(last - level)).astype(jnp.bfloat16)
        states[head] = lax.dot_general(
            key_scaled, value, (((0,), (0,)), ((), ())), preferred_element_type=jnp.float32
        )
        levels[head] = level
        growth[head] = jnp.exp(level)
        return carry

    def within(side, step, carry):
        head = side * (heads // 2) + step
        columns = pl.ds(pl.multiple_of(step * HEAD, HEAD), HEAD)
        query, key, value = (heads_in[side, which, :, columns] for which in range(3))
        scores = lax.dot_general(
            query, key, (((1,), (1,)), ((), ())), preferred_element_type=jnp.float32
        )
        gaps = jnp.minimum(levels[head] - cumulated_rows[head], 0.0)
        weights = jnp.where(causal, scores * jnp.exp(gaps), 0.0).astype(jnp.bfloat16)
        inside[head] = jnp.dot(weights, value, preferred_element_type=jnp.float32)
        return carry

    def state_wait(head):
        landing = incoming.at[head]
        pltpu.make_async_copy(landing, landing, state_recv.at[head]).wait()

    def pass_on(side):
        def step_on(step, carry):
            head = side * (heads // 2) + step

            @pl.when(place > 0)
            def _():
                state_wait(head)

            gain = growth[head, rows - 1 :, :]
            outgoing[head] = (gain * incoming[head].astype(jnp.float32) + states[head]).astype(
                jnp.bfloat16
            )
            state_copy(head).start()
            return carry

        @pl.when(has_next)
        def _():
            lax.fori_loop(0, heads // 2, step_on, 0)

    def receive_last(side):
        def step_on(step, carry):
            state_wait(side * (heads // 2) + step)
            return carry

        @pl.when((place > 0) & jnp.logical_not(has_next))
        def _():
            lax.fori_loop(0, heads // 2, step_on, 0)

    def across(side, step, carry):
        head = side * (heads // 2) + step
        columns = pl.ds(pl.multiple_of(step * HEAD, HEAD), HEAD)
        carried = jnp.dot(
            heads_in[side, 0, :, columns], incoming[head], preferred_element_type=jnp.float32
        )
        outputs = inside[head] + growth[head] * carried
        mean_square = jnp.mean(outputs * outputs, axis=1, keepdims=True)
        attended[side, :, columns] = (outputs * lax.rsqrt(mean_square + 1e-06)).astype(
            jnp.bfloat16
        )
        return carry

    @pl.when(place == 0)
    def _():
        incoming[...] = jnp.zeros(incoming.shape, incoming.dtype)

    sends = []
    if relayed(devices):
        x_peer = me + 2 - 4 * lax.rem(me // 2, 2)
        y_peer = me + 4 - 8 * (me // 4)
        corner = x_peer + y_peer - me

    def exchange(own, buffer, send_sem, recv_sem):
        count = []

        def send(source, origin, side, target):
            copy = pltpu.make_async_remote_copy(
                src_ref=source,
                dst_ref=buffer.at[origin, side],
                send_sem=send_sem.at[len(count)],
                recv_sem=recv_sem.at[origin, side],
                device_id={"ep": target},
                device_id_type=MESH,
            )
            copy.start()
            count.append(copy)
            sends.append(copy)

        def arrived(origin, side):
            landing = buffer.at[origin, side]
            pltpu.make_async_copy(landing, landing, recv_sem.at[origin, side]).wait()

        def forward(origin, side, target):
            send(buffer.at[origin, side], origin, side, target)

        def begin(side):
            if relayed(devices):
                peers = (x_peer, y_peer) if side == 0 else (y_peer, x_peer)
            else:
                peers = [lax.rem(me + 2 * step, devices) for step in range(1, pairs)]
            for peer in peers:
                send(own.at[side], me, side, peer)
            send(own.at[side], me, side, sibling)

        def take(use):
            if relayed(devices):
                arrived(x_peer, 0)
                forward(x_peer, 0, y_peer)
                forward(x_peer, 0, sibling)
                arrived(y_peer, 0)
                forward(y_peer, 0, sibling)
                arrived(y_peer, 1)
                forward(y_peer, 1, x_peer)
                forward(y_peer, 1, sibling)
                arrived(x_peer, 1)
                forward(x_peer, 1, sibling)
                arrived(sibling, 0)
                arrived(sibling, 1)

                def use_first(step, carry):
                    use(jnp.where(step == 0, sibling, jnp.where(step == 1, x_peer, y_peer)))
                    return carry

                lax.fori_loop(0, 3, use_first, 0)
                for origin in (x_peer, y_peer):
                    arrived(origin + turn, 0)
                    arrived(origin + turn, 1)

                def use_second(step, carry):
                    use(jnp.where(step == 0, x_peer, y_peer) + turn)
                    return carry

                arrived(corner, 0)
                forward(corner, 0, sibling)
                lax.fori_loop(0, 2, use_second, 0)
                arrived(corner, 1)
                forward(corner, 1, sibling)

                def use_last(step, carry):
                    origin = corner + turn * step
                    for side in range(2):
                        @pl.when(step == 1)
                        def _():
                            arrived(origin, side)
                    use(origin)
                    return carry

                lax.fori_loop(0, 2, use_last, 0)
            else:
                for step in range(1, pairs):
                    origin = lax.rem(me + devices - 2 * step, devices)
                    for side in range(2):
                        arrived(origin, side)
                        forward(origin, side, sibling)

                def use_same(step, carry):
                    use(lax.rem(me + 2 * step, devices))
                    return carry

                lax.fori_loop(1, pairs, use_same, 0)

                def use_other(step, carry):
                    origin = lax.rem(sibling + 2 * step, devices)
                    arrived(origin, 0)
                    arrived(origin, 1)
                    use(origin)
                    return carry

                lax.fori_loop(0, pairs, use_other, 0)

        return begin, take

    begin, take = exchange(attended, gathered, block_send, block_recv)
    count = heads // 2
    for side in range(2):
        for which in range(3):
            heads_copy(side, which).wait()
        lax.fori_loop(0, count, functools.partial(update, side), 0, unroll=True)
        if side == 0:
            pass_on(side)
    for side in range(2):
        if side == 1:
            pass_on(side)
        lax.fori_loop(0, count, functools.partial(within, side), 0, unroll=True)
        receive_last(side)
        lax.fori_loop(0, count, functools.partial(across, side), 0, unroll=True)
        begin(side)

    def multiplied(block, origin):
        result = None
        for side in range(2):
            columns = pl.ds(pl.multiple_of(origin * width + side * half, half), half)
            term = lax.dot_general(
                block[side],
                weight[:, columns],
                (((1,), (1,)), ((), ())),
                preferred_element_type=jnp.float32,
            )
            result = term if result is None else result + term
        return result

    load.wait()
    total[...] = multiplied(attended, me)

    def multiply(origin):
        total[...] += multiplied(gathered.at[origin], origin)

    take(multiply)

    begin, take = exchange(projected, spread_out, row_send, row_recv)
    part = rows // 2
    for side in range(2):
        projected[side] = total[side * part : (side + 1) * part, :].astype(jnp.bfloat16)
        begin(side)

    slots = lax.broadcasted_iota(jnp.int32, (capacity, rows), 0)
    named = jnp.max(jnp.where(named_ref[...] == me, 1.0, 0.0), axis=0, keepdims=True)
    earlier = jnp.where(t_index < s_index, 1.0, 0.0).astype(jnp.bfloat16)
    slot = jnp.dot(
        jnp.broadcast_to(named, (16, rows)).astype(jnp.bfloat16),
        earlier,
        preferred_element_type=jnp.float32,
    )[0:1, :]
    slot = jnp.where(named > 0.5, slot, -1.0).astype(jnp.int32)
    picked = slot == slots
    picks = jnp.where(picked, 1.0, 0.0).astype(jnp.bfloat16)
    row_number = lax.broadcasted_iota(jnp.int32, (1, rows), 1) + place * rows

    def flag(index, flags):
        return jnp.where(row_number == flagged_ref[index], 1.0, flags)

    row_flags = lax.fori_loop(
        0, flagged_ref.shape[0], flag, jnp.zeros((1, rows), jnp.float32), unroll=8
    )
    flags = jnp.sum(jnp.where(picked, row_flags, 0.0), axis=1, keepdims=True) > 0.5

    def direction_wait(step, carry):
        origin = lax.rem(me + step, devices)
        landing = directions.at[origin]
        pltpu.make_async_copy(landing, landing, direction_recv.at[origin]).wait()
        return carry

    lax.fori_loop(1, devices, direction_wait, 0)
    squares = jnp.sum(directions[...] * directions[...], axis=0)
    norm_square = jnp.sum(squares, axis=1, keepdims=True) + 1e-06

    def pick(block, origin):
        picked_rows = jnp.dot(
            picks[:, :part], block[0], preferred_element_type=jnp.float32
        ) + jnp.dot(picks[:, part:], block[1], preferred_element_type=jnp.float32)
        tiles[origin] = picked_rows.astype(jnp.bfloat16)
        return jnp.sum(picked_rows * directions[origin], axis=1, keepdims=True)

    products[...] = pick(projected, me)

    def collect(origin):
        products[...] += pick(spread_out.at[origin], origin)

    take(collect)
    gain = products[...] / norm_square

    def finish(origin, carry):
        tile = tiles[origin]
        removed = (tile.astype(jnp.float32) - gain * directions[origin]).astype(jnp.bfloat16)
        result = jnp.where(flags, removed, tile)
        if cols % 128:
            out_ref[origin] = result
        else:
            out_ref[:, pl.ds(pl.multiple_of(origin * cols, cols), cols)] = result
        return carry

    lax.fori_loop(0, devices, finish, 0)

    for copy in sends:
        copy.wait_send()

    @pl.when(has_next)
    def _():
        def state_sent(head, carry):
            state_copy(head).wait_send()
            return carry

        lax.fori_loop(0, heads, state_sent, 0)

    def sent(step, carry):
        pltpu.make_async_copy(direction_ref, direction_ref, direction_send.at[step]).wait()
        return carry

    lax.fori_loop(1, devices, sent, 0)


def layer(
    queries, key_rows, value_rows, decay, out_weight, named, flagged, direction, capacity
):
    devices = lax.axis_size("ep")
    rows, width = queries.shape
    heads = width // HEAD
    cols = out_weight.shape[0]
    copies = 16 if relayed(devices) else 2 * devices
    shape = (devices, capacity, cols) if cols % 128 else (capacity, devices * cols)
    vmem = pl.BlockSpec(memory_space=pltpu.VMEM)
    hbm = pl.BlockSpec(memory_space=pl.ANY)
    dma = pltpu.SemaphoreType.DMA
    return pl.pallas_call(
        functools.partial(layer_kernel, devices, lax.axis_size("ctx"), capacity),
        out_shape=jax.ShapeDtypeStruct(shape, jnp.bfloat16),
        in_specs=[hbm] * 3 + [vmem, hbm, vmem, pl.BlockSpec(memory_space=pltpu.SMEM), vmem],
        out_specs=vmem,
        scratch_shapes=[
            pltpu.VMEM(out_weight.shape, jnp.bfloat16),
            pltpu.VMEM((2, 3, rows, width // 2), jnp.bfloat16),
            pltpu.VMEM((heads, rows, HEAD), jnp.float32),
            pltpu.VMEM((heads, rows, 1), jnp.float32),
            pltpu.VMEM((heads, rows, 1), jnp.float32),
            pltpu.VMEM((heads, HEAD, HEAD), jnp.float32),
            pltpu.VMEM((rows, heads), jnp.float32),
            pltpu.VMEM((heads, 1, rows), jnp.float32),
            pltpu.VMEM((heads, HEAD, HEAD), jnp.bfloat16),
            pltpu.VMEM((heads, HEAD, HEAD), jnp.bfloat16),
            pltpu.VMEM((2, rows, width // 2), jnp.bfloat16),
            pltpu.VMEM((devices, 2, rows, width // 2), jnp.bfloat16),
            pltpu.VMEM((rows, cols), jnp.float32),
            pltpu.VMEM((2, rows // 2, cols), jnp.bfloat16),
            pltpu.VMEM((devices, 2, rows // 2, cols), jnp.bfloat16),
            pltpu.VMEM((devices, capacity, cols), jnp.bfloat16),
            pltpu.VMEM((capacity, 1), jnp.float32),
            pltpu.VMEM((devices, 1, cols), jnp.float32),
            dma,
            dma((2, 3)),
            dma((heads,)),
            dma((heads,)),
            dma((copies,)),
            dma((devices, 2)),
            dma((copies,)),
            dma((devices, 2)),
            dma((devices,)),
            dma((devices,)),
        ],
        compiler_params=pltpu.CompilerParams(
            collective_id=0, has_side_effects=True, vmem_limit_bytes=44 * 1024 * 1024
        ),
        cost_estimate=pl.CostEstimate(
            flops=2 * rows * devices * width * cols, bytes_accessed=out_weight.size * 2,
            transcendentals=0,
        ),
    )(queries, key_rows, value_rows, decay, out_weight, named, flagged, direction)


def local(queries, key_rows, value_rows, log_decay, out_weight, expert_ids, flagged, direction):
    block_rows = queries.shape[0]
    assert block_rows == SUB
    experts_all = lax.axis_size("ep") * EXP_DEV
    capacity = 2 * block_rows * TOP // experts_all
    tiles = layer(
        queries,
        key_rows,
        value_rows,
        log_decay.T,
        out_weight,
        expert_ids.T,
        flagged,
        direction[None, :],
        capacity,
    )
    if tiles.ndim == 3:
        tiles = jnp.transpose(tiles, (1, 0, 2)).reshape(capacity, -1)
    return tiles[None]


def solution(mesh):
    placed = (
        P("ctx", "ep"),
        P("ctx", "ep"),
        P("ctx", "ep"),
        P("ctx", "ep"),
        P("ep", None),
        P("ctx", None),
        P("ctx"),
        P("ep"),
    )
    return jax.shard_map(
        local, mesh=mesh, in_specs=placed, out_specs=P("ep", "ctx", None), check_vma=False
    )
```
